32 devices in a mesh: grp: 4 (over y, x), dp: 8 (over z, core).
Axes of the slice: x: 2, y: 2, z: 4, core: 2. Of those that a mesh axis runs over, the one named last changes fastest.
Arguments:
- queries: bfloat16 [4096, 2048], P(('grp', 'dp')), parts along dimension 0, may hold values from -96 to 96
- new_keys: bfloat16 [4096, 256], P(('grp', 'dp')), parts along dimension 0, may hold values from -5 to 5
- new_values: bfloat16 [4096, 256], P(('grp', 'dp')), parts along dimension 0, may hold values from -5 to 5
- cache_keys: bfloat16 [32768, 256], P(('grp', 'dp')), parts along dimension 0, may hold values from -5 to 5
- cache_values: bfloat16 [32768, 256], P(('grp', 'dp')), parts along dimension 0, may hold values from -5 to 5
- prefix_len: int32 [32], P(('grp', 'dp')), parts along dimension 0, may hold values from 1 to 1024, 4096 in all
- residual: bfloat16 [4096, 2048], P(('grp', 'dp')), parts along dimension 0, may hold values from -3 to 3
- out_weight: bfloat16 [2048, 2048], P('dp'), may hold values from -0.125 to 0.125
- norm_gain: float32 [2048], replicated, may hold values from 0.1 to 1.9
- expert_ids: int32 [4096, 4], P(('grp', 'dp')), parts along dimension 0, may hold values from 0 to 7, all different within a row; in each aligned block of 128 rows (0 to 127, 128 to 255, ...) at most 72 rows name the same one
- gate_scores: float32 [4096, 4], P(('grp', 'dp')), parts along dimension 0, may hold values from 0.05 to 1
- expert_gate_up: bfloat16 [8, 2048, 1536], P('dp'), may hold values from -0.125 to 0.125
- expert_down: bfloat16 [8, 768, 2048], P('dp'), may hold values from -0.21875 to 0.21875
Outputs:
- mixed: bfloat16 [4096, 2048], P(('grp', 'dp')), parts along dimension 0
The draws below stay inside these ranges and needn't reach their ends.
There are 4 independent parts, one for each index of `grp`. The reference program is written for one: setup_inputs(seed, part) draws one part's arguments, and reference() takes and returns one part's arrays. A program takes and returns all parts, laid end to end along the dimension named above; an argument that names none is the same for every part. Nothing has to cross between parts.
Inputs may be any that keep to these rules, and one draw needn't show every extreme that they name: `expert_ids`: among the rows of one device each expert is named by at most 72 rows.
All inputs are finite; a program needn't handle non-finite values. No bound on the sum of `prefix_len` on one device may be relied on, other than what follows from the above.
Results may differ from the reference program's by a relative error of at most 0.0095.
Values may be sent and summed in bfloat16 or wider, within the bound.
A program may use at most 128 MiB of HBM per device.

```python
import math
import jax
import jax.numpy as jnp
import numpy as np
from jax import lax

D = 2048
HQ = 16
HK = 2
HD = 128
FF = 768
TOKENS_PER_SHARD = 128
PMAX = 1024
EXPERTS = 8
TOPK = 4
MOST = 72
TOKENS = 1024
N_DP = 8


def anchor_keys(key):
    base = jax.random.normal(key, (TOKENS // TOKENS_PER_SHARD * PMAX, HK * HD), jnp.float32)
    return jnp.clip(base, -4.5, 4.5)


def draw_cache_keys(key, part):
    keys = anchor_keys(key)
    return keys.astype(jnp.bfloat16)


def draw_queries(key, part):
    key = jax.random.fold_in(key, 3)
    first = jax.random.fold_in(key, 0)
    values = 2.0 * jnp.clip(jax.random.normal(first, (TOKENS, HQ * HD), jnp.float32), -4.0, 4.0)
    return values.astype(jnp.bfloat16)


def block_scale(own_key, extent, pieces, least, top_value):
    factor_of = 1.0
    for dim, shards_of in pieces:
        heights = jax.random.uniform(jax.random.fold_in(jax.random.fold_in(own_key, 6), dim), (shards_of,), jnp.float32, least / len(pieces), top_value / len(pieces))
        factor_of = factor_of * jnp.repeat(jnp.exp(heights), extent[dim] // shards_of).reshape((-1,) + (1,) * (len(extent) - 1 - dim))
    return factor_of


def split_up(number_of, total, limit, slope):
    loads = [(1 << 20) // math.isqrt(rank ** slope) + 1 for rank in range(2, number_of + 1)]
    surplus, counts = total - limit - (number_of - 1), [1] * (number_of - 1)
    while surplus > 0:
        movable = [i for i in range(number_of - 1) if counts[i] < limit]
        whole, remaining = sum([loads[i] for i in movable]), surplus
        for i in movable:
            addition = min(limit - counts[i], max(1, remaining * loads[i] // whole), surplus)
            counts[i] = counts[i] + addition
            surplus = surplus - addition
    return np.array([limit] + counts)


def uneven_parts(own_key, number_of, total, limit, lean):
    if number_of == 2:
        one = jax.random.randint(own_key, (), max(1, total - limit), min(limit, total - 1) + 1)
        return jnp.stack([one, total - one])
    tallies = jnp.asarray(split_up(number_of, total, limit, lean), jnp.int32)
    pairs = (number_of - 1) // 2
    giver, sink = tallies[1:1 + 2 * pairs:2], tallies[2:2 + 2 * pairs:2]
    room = jnp.minimum(giver - 1, limit - sink)
    passed = jax.random.randint(jax.random.fold_in(own_key, 1), (pairs,), 0, 1 << 20) % (room + 1)
    tallies = tallies.at[1:1 + 2 * pairs:2].set(giver - passed).at[2:2 + 2 * pairs:2].set(sink + passed)
    return tallies[jax.random.permutation(jax.random.fold_in(own_key, 2), number_of)]


def deal_out(stream_key, own, number, rows, amount, top, limit, lean):
    order = jax.random.permutation(stream_key, amount)
    crowded, usual = shares(amount, rows * top, limit, lean, True), shares(amount, rows * top, limit, lean, False)
    places = jnp.arange(amount)

    def named(lengths, turn):
        used = int((lengths > 0).sum())
        fixed = max(1, used // 4)
        passed = fixed + (places - fixed + turn * (used - fixed)) % max(1, amount - fixed)
        return jnp.zeros((amount,), jnp.int32).at[order[jnp.where(places < fixed, places, passed)]].set(jnp.asarray(lengths, jnp.int32))

    lengths = jnp.where(number % 4 == 0, named(crowded, number // 4), named(usual, number - number // 4 - 1))
    mixed = jax.random.permutation(jax.random.fold_in(own, 3), amount)
    giver, taker = mixed[0:amount // 2 * 2:2], mixed[1:amount // 2 * 2:2]
    margin = jnp.minimum(lengths[giver] - 1, limit - lengths[taker]) // 2
    margin = jnp.where((giver == order[0]) | (taker == order[0]) | (lengths[taker] == 0), 0, jnp.maximum(margin, 0))
    passed = jax.random.randint(jax.random.fold_in(own, 4), (amount // 2,), 0, 1 << 20) % (margin + 1)
    lengths = lengths.at[giver].add(-passed).at[taker].add(passed)
    items = jnp.searchsorted(jnp.cumsum(lengths), jnp.arange(rows * top), side="right").astype(jnp.int32)
    listing = items.reshape(top, rows).T
    listing = listing[jax.random.permutation(jax.random.fold_in(own, 1), rows)]
    turn = jax.random.randint(jax.random.fold_in(own, 2), (rows, 1), 0, top)
    return jnp.take_along_axis(listing, (jnp.arange(top)[None, :] + turn) % top, axis=1)


def shares(count, total, reach, slope, full):
    weights = [(1 << 20) // math.isqrt(grade ** slope) + 1 for grade in range(1, count + 1)]
    largest = reach if full else min(reach, max(-(-total // count), total * weights[0] // sum(weights)))
    least = 1 if total - largest >= count - 1 else 0
    given, spare = [largest] + [least] * (count - 1), total - largest - least * (count - 1)
    while spare > 0:
        movable = [i for i in range(1, count) if given[i] < largest] or [i for i in range(1, count) if given[i] < reach]
        mass, left = sum([weights[i] for i in movable]), spare
        for i in movable:
            extra = min(reach - given[i], max(1, left * weights[i] // mass), spare)
            given[i] = given[i] + extra
            spare = spare - extra
    return np.array(given)


def centred(stream_key, dims, spread, bound, shards=(), kind=jnp.bfloat16):
    array = spread * jax.random.normal(stream_key, dims, jnp.float32)
    if shards:
        array = array * block_scale(stream_key, dims, shards, -0.22, 0.18)
    return jnp.clip(array, -bound, bound).astype(kind)


def setup_inputs(seed: int = 0, part: int = 0) -> dict:
    key_of = jax.random.split(jax.random.key(seed), 14)
    part_splits = jax.random.split(jax.random.fold_in(key_of[13], part), 14)
    queries = draw_queries(jax.random.fold_in(jax.random.fold_in(key_of[13], part), 71), part)
    new_keys = centred(part_splits[1], (TOKENS, HK * HD), 1.0, 5.0, ((0, 8),))
    new_values = centred(part_splits[2], (TOKENS, HK * HD), 1.0, 5.0, ((0, 8),))
    cache_keys = draw_cache_keys(jax.random.fold_in(jax.random.fold_in(key_of[13], part), 71), part)
    cache_values = centred(part_splits[4], (N_DP * PMAX, HK * HD), 1.0, 5.0, ((0, 8),))
    prefix_len = uneven_parts(part_splits[5], N_DP, N_DP * PMAX // 2, PMAX, 2).astype(jnp.int32)
    residual = centred(part_splits[6], (TOKENS, D), 0.5, 3.0, ((0, 8),))
    out_weight = centred(key_of[7], (HQ * HD, D), (HQ * HD) ** -0.5, 0.125, ((0, 8),))
    norm_gain = jnp.clip(1.0 + 0.18 * jax.random.normal(key_of[8], (D,), jnp.float32), 0.1, 1.9)
    expert_ids_keys = jax.random.split(jax.random.fold_in(part_splits[9], 1), TOKENS // TOKENS_PER_SHARD)
    expert_ids_turns = jax.random.permutation(jax.random.fold_in(part_splits[9], 3), TOKENS // TOKENS_PER_SHARD)
    expert_ids = jax.vmap(lambda own, number: deal_out(jax.random.fold_in(part_splits[9], 2), own, number, TOKENS_PER_SHARD, EXPERTS, TOPK, MOST, 2))(expert_ids_keys, expert_ids_turns).reshape((TOKENS, TOPK))
    gate_scores = jnp.clip(jnp.exp(math.log(1.0) - 2.9957323 * jax.random.uniform(part_splits[10], (TOKENS, TOPK), jnp.float32) ** block_scale(part_splits[10], (TOKENS, TOPK), ((0, 8),), -0.2, 0.2)), 0.05, 1.0)
    expert_gate_up = centred(key_of[11], (EXPERTS, D, 2 * FF), D ** -0.5, 0.125, ((0, 8),))
    expert_down = centred(key_of[12], (EXPERTS, FF, D), FF ** -0.5, 0.21875, ((0, 8),))
    return dict(queries=queries, new_keys=new_keys, new_values=new_values, cache_keys=cache_keys, cache_values=cache_values, prefix_len=prefix_len, residual=residual, out_weight=out_weight, norm_gain=norm_gain, expert_ids=expert_ids, gate_scores=gate_scores, expert_gate_up=expert_gate_up, expert_down=expert_down)


NEGATIVE_FILL = -1e+30

def attend(q, new_k, new_v, cache_k, cache_v, plen):
    tok = q.shape[0]
    qh = q.reshape(tok, HK, HQ // HK, HD).astype(jnp.float32)
    keys = jnp.concatenate([cache_k, new_k], axis=0).reshape(-1, HK, HD).astype(jnp.float32)
    vals = jnp.concatenate([cache_v, new_v], axis=0).reshape(-1, HK, HD).astype(jnp.float32)
    router_logits = jnp.einsum('tgqd,kgd->tgqk', qh, keys) * HD ** (-0.5)
    position = jnp.arange(PMAX + tok, dtype=jnp.int32)
    row = jnp.arange(tok, dtype=jnp.int32)
    valid_positions = (position[None, :] < plen) | (position[None, :] >= PMAX) & (position[None, :] - PMAX <= row[:, None])
    validity_mask = valid_positions[:, None, None, :]
    router_logits = jnp.where(validity_mask, router_logits, NEGATIVE_FILL)
    top_choice = lax.optimization_barrier(jnp.max(router_logits, axis=-1))
    expert_probabilities = jnp.where(validity_mask, jnp.exp(router_logits - top_choice[..., None]), 0.0)
    total = lax.optimization_barrier(jnp.sum(expert_probabilities, axis=-1))
    rounded = lax.optimization_barrier(expert_probabilities.astype(jnp.bfloat16)).astype(jnp.float32)
    summed = jnp.einsum('tgqk,kgd->tgqd', rounded, vals)
    return (summed / total[..., None]).reshape(tok, HQ * HD).astype(jnp.bfloat16)

def reference(queries, new_keys, new_values, cache_keys, cache_values, prefix_len, residual, out_weight, norm_gain, expert_ids, gate_scores, expert_gate_up, expert_down):
    packed = (queries.reshape(N_DP, TOKENS_PER_SHARD, HQ * HD), new_keys.reshape(N_DP, TOKENS_PER_SHARD, HK * HD), new_values.reshape(N_DP, TOKENS_PER_SHARD, HK * HD), cache_keys.reshape(N_DP, PMAX, HK * HD), cache_values.reshape(N_DP, PMAX, HK * HD), prefix_len)
    attended = lax.map(lambda item: attend(*item), packed).reshape(TOKENS, HQ * HD)
    projected = jnp.dot(attended, out_weight, preferred_element_type=jnp.float32)
    hidden_state = residual.astype(jnp.float32) + projected
    scale = lax.rsqrt(lax.optimization_barrier(jnp.mean(hidden_state * hidden_state, axis=-1, keepdims=True)) + 1e-06)
    normed = (hidden_state * scale * norm_gain).astype(jnp.bfloat16)
    route_weights = gate_scores / lax.optimization_barrier(jnp.sum(gate_scores, axis=-1, keepdims=True))

    def expert_step(total, index):
        pair = jnp.dot(normed, expert_gate_up[index], preferred_element_type=jnp.float32)
        act = (jax.nn.silu(pair[:, :FF]) * pair[:, FF:]).astype(jnp.bfloat16)
        out = jnp.dot(act, expert_down[index], preferred_element_type=jnp.float32).astype(jnp.bfloat16)
        share = lax.optimization_barrier(jnp.sum(jnp.where(expert_ids == index, route_weights, 0.0), axis=-1))
        return (total + share[:, None] * out.astype(jnp.float32), None)
    total, _ = lax.scan(expert_step, jnp.zeros((TOKENS, D), jnp.float32), jnp.arange(EXPERTS, dtype=jnp.int32))
    return (hidden_state + total).astype(jnp.bfloat16)
```

```python
import functools

import jax
import jax.numpy as jnp
from jax import lax
from jax.experimental import pallas as pl
from jax.experimental.pallas import tpu as pltpu
from jax.sharding import PartitionSpec as P

D = 2048
HQ = 16
HK = 2
HD = 128
FF = 768
BLK = 256


NEGATIVE_FILL = -1e30


def block_step(state, query_heads, keys, vals, mask):
    top_old, sum_old, acc_old = state
    router_logits = jnp.einsum(
        "tgqd,kgd->tgqk", query_heads, keys, preferred_element_type=jnp.float32
    ) * HD ** (-0.5)
    wide_mask = mask[:, None, None, :]
    router_logits = jnp.where(wide_mask, router_logits, NEGATIVE_FILL)
    top_new = jnp.maximum(top_old, jnp.max(router_logits, axis=-1))
    expert_probabilities = jnp.where(wide_mask, jnp.exp(router_logits - top_new[..., None]), 0.0)
    shrink = jnp.exp(top_old - top_new)
    sum_new = sum_old * shrink + jnp.sum(expert_probabilities, axis=-1)
    acc_new = acc_old * shrink[..., None] + jnp.einsum(
        "tgqk,kgd->tgqd",
        expert_probabilities.astype(jnp.bfloat16),
        vals,
        preferred_element_type=jnp.float32,
    )
    return (top_new, sum_new, acc_new)


def prefix_range(state, query_heads, cache_k, cache_v, low, high):
    first = low // BLK
    last = (high + BLK - 1) // BLK

    def step(index, carry):
        start = index * BLK
        keys = lax.dynamic_slice_in_dim(cache_k, start, BLK, 0).reshape(BLK, HK, HD)
        vals = lax.dynamic_slice_in_dim(cache_v, start, BLK, 0).reshape(BLK, HK, HD)
        position = start + jnp.arange(BLK, dtype=jnp.int32)
        mask = ((position >= low) & (position < high))[None, :]
        return block_step(carry, query_heads, keys, vals, mask)

    return lax.fori_loop(first, last, step, state)


def empty_state(tok):
    group = HQ // HK
    return (
        jnp.full((tok, HK, group), NEGATIVE_FILL, jnp.float32),
        jnp.zeros((tok, HK, group), jnp.float32),
        jnp.zeros((tok, HK, group, HD), jnp.float32),
    )


SPLIT = 2
VMEM_BYTES = 58 * 1024 * 1024


def block_at(p, z, nz):
    both = jnp.minimum(z, nz - 1 - z)
    half = (p + 1) // 2
    near = jnp.where(p % 2 == 1, z - half, z + half)
    far = jnp.where(z > nz - 1 - z, z - (p - both), z + (p - both))
    return jnp.where(p <= 2 * both, near, far)


def experts_kernel(
    nz, split, x_ref, hidden_ref, share_ref, gu_hbm, down_hbm, out_ref,
    gu, down, xs, ys, sib_sum, line_sum, total, act, acc,
    load_sem, x_send, x_recv, xsib_send, xsib_recv, ysib_send, ysib_recv, line_send, line_recv,
):
    me = lax.axis_index("dp")
    z, c = me // 2, me % 2
    other = 1 - c
    sibling = 2 * z + other
    right, left = me + 2, me - 2
    rows = xs.shape[3]
    width = xs.shape[4]
    hidden_units = down.shape[0]
    has_left, has_right = z > 0, z < nz - 1

    load_gu = pltpu.make_async_copy(gu_hbm, gu, load_sem.at[0])
    load_down = pltpu.make_async_copy(down_hbm, down, load_sem.at[1])
    load_gu.start()
    load_down.start()
    for s in range(split):
        xs[z, s, c] = x_ref[s]

    barrier = pltpu.get_barrier_semaphore()

    def greet(device):
        pl.semaphore_signal(
            barrier, inc=1, device_id={"dp": device}, device_id_type=pl.DeviceIdType.MESH
        )

    greet(sibling)
    pl.when(has_left)(lambda: greet(left))
    pl.when(has_right)(lambda: greet(right))
    pl.semaphore_wait(barrier, 1 + jnp.where(has_left, 1, 0) + jnp.where(has_right, 1, 0))

    def remote(src, dst, send, recv, device):
        return pltpu.make_async_remote_copy(
            src_ref=src, dst_ref=dst, send_sem=send, recv_sem=recv,
            device_id={"dp": device}, device_id_type=pl.DeviceIdType.MESH,
        )

    def x_line(b, s, way, device):
        return remote(xs.at[b, s, c], xs.at[b, s, c], x_send.at[way, b, s], x_recv.at[b, s], device)

    def x_sib(b, s, core):
        return remote(
            xs.at[b, s, core], xs.at[b, s, core], xsib_send.at[b, s], xsib_recv.at[b, s], sibling
        )

    def y_sib(b, s):
        return remote(
            ys.at[b, s, other], sib_sum.at[b, s], ysib_send.at[b, s], ysib_recv.at[b, s], sibling
        )

    def sum_line(b, s, way, device):
        return remote(
            total.at[b, s], line_sum.at[way, b, s], line_send.at[b, s], line_recv.at[way, b, s], device
        )

    def send_own(s, carry):
        pl.when(has_right)(lambda: x_line(z, s, 0, right).start())
        pl.when(has_left)(lambda: x_line(z, s, 1, left).start())
        x_sib(z, s, c).start()
        return carry

    lax.fori_loop(0, split, send_own, 0)
    load_gu.wait()
    load_down.wait()

    def send_sum(b, s):
        pl.when(b > z)(lambda: sum_line(b, s, 0, right).start())
        pl.when(b < z)(lambda: sum_line(b, s, 1, left).start())

    def is_end(b):
        return ((b > z) & (z == 0)) | ((b < z) & (z == nz - 1))

    def compute(i, carry):
        p, s = i // split, i % split
        b = block_at(p, z, nz)

        @pl.when(p > 0)
        def _():
            x_line(b, s, 0, sibling).wait_recv()
            pl.when((b < z) & has_right)(lambda: x_line(b, s, 0, right).start())
            pl.when((b > z) & has_left)(lambda: x_line(b, s, 1, left).start())
            x_sib(b, s, c).start()

        x_sib(b, s, other).wait_recv()
        x = xs[b, s].reshape(2 * rows, width)
        tile = 256
        for f in range(0, hidden_units, tile):
            gate = jnp.dot(x, gu[:, f : f + tile], preferred_element_type=jnp.float32)
            up = jnp.dot(
                x, gu[:, hidden_units + f : hidden_units + f + tile],
                preferred_element_type=jnp.float32,
            )
            act[:, f : f + tile] = (gate / (1.0 + jnp.exp(-gate)) * up).astype(jnp.bfloat16)
        share = share_ref[b, s]
        for d in range(0, width, 512):
            y = jnp.dot(act[...], down[:, d : d + 512], preferred_element_type=jnp.float32)
            ys[b, s, :, :, d : d + 512] = (
                (y * share).astype(jnp.bfloat16).reshape(2, rows, 512)
            )
        y_sib(b, s).start()

        @pl.when(is_end(b))
        def _():
            y_sib(b, s).wait_recv()
            total[b, s] = (
                ys[b, s, c].astype(jnp.float32) + sib_sum[b, s].astype(jnp.float32)
            ).astype(jnp.bfloat16)
            send_sum(b, s)

        return carry

    lax.fori_loop(0, nz * split, compute, 0)

    def add_and_pass(b, s, way):
        y_sib(b, s).wait_recv()
        sum_line(b, s, way, sibling).wait_recv()
        total[b, s] = (
            ys[b, s, c].astype(jnp.float32)
            + sib_sum[b, s].astype(jnp.float32)
            + line_sum[way, b, s].astype(jnp.float32)
        ).astype(jnp.bfloat16)
        send_sum(b, s)

    def pass_on(i, carry):
        hop, s = i // split, i % split
        from_left, from_right = hop - z, 2 * (nz - 1) - z - hop
        pl.when(has_left & (from_left > z) & (from_left < nz))(lambda: add_and_pass(from_left, s, 0))
        pl.when(has_right & (from_right < z) & (from_right >= 0))(
            lambda: add_and_pass(from_right, s, 1)
        )
        return carry

    lax.fori_loop(split, (2 * nz - 1) * split, pass_on, 0)

    def finish(s, carry):
        y_sib(z, s).wait_recv()
        acc[...] = (
            hidden_ref[s] + ys[z, s, c].astype(jnp.float32) + sib_sum[z, s].astype(jnp.float32)
        )

        @pl.when(has_left)
        def _():
            sum_line(z, s, 0, sibling).wait_recv()
            acc[...] += line_sum[0, z, s].astype(jnp.float32)

        @pl.when(has_right)
        def _():
            sum_line(z, s, 1, sibling).wait_recv()
            acc[...] += line_sum[1, z, s].astype(jnp.float32)

        out_ref[s] = acc[...].astype(out_ref.dtype)
        return carry

    lax.fori_loop(0, split, finish, 0)

    def drain(i, carry):
        b, s = i // split, i % split
        pl.when((b <= z) & has_right)(lambda: x_line(b, s, 0, right).wait_send())
        pl.when((b >= z) & has_left)(lambda: x_line(b, s, 1, left).wait_send())
        x_sib(b, s, c).wait_send()
        y_sib(b, s).wait_send()
        pl.when(b != z)(lambda: sum_line(b, s, 0, sibling).wait_send())
        return carry

    lax.fori_loop(0, nz * split, drain, 0)


def experts(normed, hidden_state, share, gate_up, down):
    tok, width = normed.shape
    n_dp = lax.axis_size("dp")
    nz, split = n_dp // 2, SPLIT
    rows = tok // split
    units = down.shape[0]
    share = share.reshape(nz, 2, split, rows).transpose(0, 2, 1, 3).reshape(nz, split, 2 * rows, 1)
    vmem = pl.BlockSpec(memory_space=pltpu.VMEM)
    hbm = pl.BlockSpec(memory_space=pl.ANY)
    half = jnp.bfloat16
    dma = pltpu.SemaphoreType.DMA
    out = pl.pallas_call(
        functools.partial(experts_kernel, nz, split),
        out_shape=jax.ShapeDtypeStruct((split, rows, width), half),
        in_specs=[vmem, vmem, vmem, hbm, hbm],
        out_specs=vmem,
        scratch_shapes=[
            pltpu.VMEM(gate_up.shape, half),
            pltpu.VMEM(down.shape, half),
            pltpu.VMEM((nz, split, 2, rows, width), half),
            pltpu.VMEM((nz, split, 2, rows, width), half),
            pltpu.VMEM((nz, split, rows, width), half),
            pltpu.VMEM((2, nz, split, rows, width), half),
            pltpu.VMEM((nz, split, rows, width), half),
            pltpu.VMEM((2 * rows, units), half),
            pltpu.VMEM((rows, width), jnp.float32),
            dma((2,)),
            dma((2, nz, split)),
            dma((nz, split)),
            dma((nz, split)),
            dma((nz, split)),
            dma((nz, split)),
            dma((nz, split)),
            dma((nz, split)),
            dma((2, nz, split)),
        ],
        compiler_params=pltpu.CompilerParams(
            collective_id=1, has_side_effects=True, vmem_limit_bytes=VMEM_BYTES
        ),
        name="experts",
    )(
        normed.reshape(split, rows, width),
        hidden_state.reshape(split, rows, width),
        share, gate_up, down,
    )
    return out.reshape(tok, width)


def local(
    queries,
    new_keys,
    new_values,
    cache_keys,
    cache_values,
    prefix_len,
    residual,
    out_weight,
    norm_gain,
    expert_ids,
    gate_scores,
    expert_gate_up,
    expert_down,
):
    tok = queries.shape[0]
    group = HQ // HK
    query_heads = queries.reshape(tok, HK, group, HD)
    plen = prefix_len[0]
    state = prefix_range(
        empty_state(tok), query_heads, cache_keys, cache_values, jnp.int32(0), plen
    )
    row = jnp.arange(tok, dtype=jnp.int32)
    causal = row[None, :] <= row[:, None]
    state = block_step(
        state, query_heads, new_keys.reshape(tok, HK, HD), new_values.reshape(tok, HK, HD), causal
    )
    attended = (state[2] / state[1][..., None]).reshape(tok, HQ * HD).astype(jnp.bfloat16)
    projected = jnp.dot(
        attended,
        lax.all_gather(out_weight, "dp", axis=0, tiled=True),
        preferred_element_type=jnp.float32,
    )
    hidden_state = residual.astype(jnp.float32) + projected
    scale = lax.rsqrt(jnp.mean(hidden_state * hidden_state, axis=-1, keepdims=True) + 1e-06)
    normed = (hidden_state * scale * norm_gain).astype(jnp.bfloat16)
    count = expert_gate_up.shape[0] * lax.axis_size("dp")
    route_weights = gate_scores / jnp.sum(gate_scores, axis=-1, keepdims=True)
    chosen = expert_ids[:, :, None] == jnp.arange(count, dtype=jnp.int32)
    share = jnp.sum(jnp.where(chosen, route_weights[:, :, None], 0.0), axis=1)
    shares = lax.all_gather(share, "dp", axis=0, tiled=True)
    mine = jnp.arange(count, dtype=jnp.int32) == lax.axis_index("dp")
    share = jnp.sum(jnp.where(mine, shares, 0.0), axis=1)
    return experts(normed, hidden_state, share, expert_gate_up[0], expert_down[0])


def solution(mesh):
    in_specs = (
        P(("grp", "dp"), None),
        P(("grp", "dp"), None),
        P(("grp", "dp"), None),
        P(("grp", "dp"), None),
        P(("grp", "dp"), None),
        P(("grp", "dp")),
        P(("grp", "dp"), None),
        P("dp", None),
        P(),
        P(("grp", "dp"), None),
        P(("grp", "dp"), None),
        P("dp", None, None),
        P("dp", None, None),
    )
    out_specs = P(("grp", "dp"), None)
    return jax.shard_map(local, mesh=mesh, in_specs=in_specs, out_specs=out_specs, check_vma=False)
```

```python
import functools

import jax
import jax.numpy as jnp
from jax import lax
from jax.experimental import pallas as pl
from jax.experimental.pallas import tpu as pltpu
from jax.sharding import PartitionSpec as P

D = 2048
HQ = 16
HK = 2
HD = 128
FF = 768
NEGATIVE_FILL = -1e30
SPLIT = 2
VMEM_BYTES = 58 * 1024 * 1024


def block_at(p, z, nz):
    both = jnp.minimum(z, nz - 1 - z)
    half = (p + 1) // 2
    near = jnp.where(p % 2 == 1, z - half, z + half)
    far = jnp.where(z > nz - 1 - z, z - (p - both), z + (p - both))
    return jnp.where(p <= 2 * both, near, far)


def experts_kernel(
    nz, split, x_ref, hidden_ref, share_ref, gu_hbm, down_hbm, out_ref,
    gu, down, xs, ys, sib_sum, line_sum, total, act, acc,
    load_sem, x_send, x_recv, xsib_send, xsib_recv, ysib_send, ysib_recv, line_send, line_recv,
):
    me = lax.axis_index("dp")
    z, c = me // 2, me % 2
    other = 1 - c
    sibling = 2 * z + other
    right, left = me + 2, me - 2
    rows = xs.shape[3]
    width = xs.shape[4]
    hidden_units = down.shape[0]
    has_left, has_right = z > 0, z < nz - 1

    load_gu = pltpu.make_async_copy(gu_hbm, gu, load_sem.at[0])
    load_down = pltpu.make_async_copy(down_hbm, down, load_sem.at[1])
    load_gu.start()
    load_down.start()
    for s in range(split):
        xs[z, s, c] = x_ref[s]

    barrier = pltpu.get_barrier_semaphore()

    def greet(device):
        pl.semaphore_signal(
            barrier, inc=1, device_id={"dp": device}, device_id_type=pl.DeviceIdType.MESH
        )

    greet(sibling)
    pl.when(has_left)(lambda: greet(left))
    pl.when(has_right)(lambda: greet(right))
    pl.semaphore_wait(barrier, 1 + jnp.where(has_left, 1, 0) + jnp.where(has_right, 1, 0))

    def remote(src, dst, send, recv, device):
        return pltpu.make_async_remote_copy(
            src_ref=src, dst_ref=dst, send_sem=send, recv_sem=recv,
            device_id={"dp": device}, device_id_type=pl.DeviceIdType.MESH,
        )

    def x_line(b, s, way, device):
        return remote(xs.at[b, s, c], xs.at[b, s, c], x_send.at[way, b, s], x_recv.at[b, s], device)

    def x_sib(b, s, core):
        return remote(
            xs.at[b, s, core], xs.at[b, s, core], xsib_send.at[b, s], xsib_recv.at[b, s], sibling
        )

    def y_sib(b, s):
        return remote(
            ys.at[b, s, other], sib_sum.at[b, s], ysib_send.at[b, s], ysib_recv.at[b, s], sibling
        )

    def sum_line(b, s, way, device):
        return remote(
            total.at[b, s], line_sum.at[way, b, s], line_send.at[b, s], line_recv.at[way, b, s], device
        )

    def send_own(s, carry):
        pl.when(has_right)(lambda: x_line(z, s, 0, right).start())
        pl.when(has_left)(lambda: x_line(z, s, 1, left).start())
        x_sib(z, s, c).start()
        return carry

    lax.fori_loop(0, split, send_own, 0)
    load_gu.wait()
    load_down.wait()

    def send_sum(b, s):
        pl.when(b > z)(lambda: sum_line(b, s, 0, right).start())
        pl.when(b < z)(lambda: sum_line(b, s, 1, left).start())

    def is_end(b):
        return ((b > z) & (z == 0)) | ((b < z) & (z == nz - 1))

    def compute(i, carry):
        p, s = i // split, i % split
        b = block_at(p, z, nz)

        @pl.when(p > 0)
        def _():
            x_line(b, s, 0, sibling).wait_recv()
            pl.when((b < z) & has_right)(lambda: x_line(b, s, 0, right).start())
            pl.when((b > z) & has_left)(lambda: x_line(b, s, 1, left).start())
            x_sib(b, s, c).start()

        x_sib(b, s, other).wait_recv()
        x = xs[b, s].reshape(2 * rows, width)
        tile = 256
        for f in range(0, hidden_units, tile):
            gate = jnp.dot(x, gu[:, f : f + tile], preferred_element_type=jnp.float32)
            up = jnp.dot(
                x, gu[:, hidden_units + f : hidden_units + f + tile],
                preferred_element_type=jnp.float32,
            )
            act[:, f : f + tile] = (gate / (1.0 + jnp.exp(-gate)) * up).astype(jnp.bfloat16)
        share = share_ref[b, s]
        for d in range(0, width, 512):
            y = jnp.dot(act[...], down[:, d : d + 512], preferred_element_type=jnp.float32)
            ys[b, s, :, :, d : d + 512] = (
                (y * share).astype(jnp.bfloat16).reshape(2, rows, 512)
            )
        y_sib(b, s).start()

        @pl.when(is_end(b))
        def _():
            y_sib(b, s).wait_recv()
            total[b, s] = (
                ys[b, s, c].astype(jnp.float32) + sib_sum[b, s].astype(jnp.float32)
            ).astype(jnp.bfloat16)
            send_sum(b, s)

        return carry

    lax.fori_loop(0, nz * split, compute, 0)

    def add_and_pass(b, s, way):
        y_sib(b, s).wait_recv()
        sum_line(b, s, way, sibling).wait_recv()
        total[b, s] = (
            ys[b, s, c].astype(jnp.float32)
            + sib_sum[b, s].astype(jnp.float32)
            + line_sum[way, b, s].astype(jnp.float32)
        ).astype(jnp.bfloat16)
        send_sum(b, s)

    def pass_on(i, carry):
        hop, s = i // split, i % split
        from_left, from_right = hop - z, 2 * (nz - 1) - z - hop
        pl.when(has_left & (from_left > z) & (from_left < nz))(lambda: add_and_pass(from_left, s, 0))
        pl.when(has_right & (from_right < z) & (from_right >= 0))(
            lambda: add_and_pass(from_right, s, 1)
        )
        return carry

    lax.fori_loop(split, (2 * nz - 1) * split, pass_on, 0)

    def finish(s, carry):
        y_sib(z, s).wait_recv()
        acc[...] = (
            hidden_ref[s] + ys[z, s, c].astype(jnp.float32) + sib_sum[z, s].astype(jnp.float32)
        )

        @pl.when(has_left)
        def _():
            sum_line(z, s, 0, sibling).wait_recv()
            acc[...] += line_sum[0, z, s].astype(jnp.float32)

        @pl.when(has_right)
        def _():
            sum_line(z, s, 1, sibling).wait_recv()
            acc[...] += line_sum[1, z, s].astype(jnp.float32)

        out_ref[s] = acc[...].astype(out_ref.dtype)
        return carry

    lax.fori_loop(0, split, finish, 0)

    def drain(i, carry):
        b, s = i // split, i % split
        pl.when((b <= z) & has_right)(lambda: x_line(b, s, 0, right).wait_send())
        pl.when((b >= z) & has_left)(lambda: x_line(b, s, 1, left).wait_send())
        x_sib(b, s, c).wait_send()
        y_sib(b, s).wait_send()
        pl.when(b != z)(lambda: sum_line(b, s, 0, sibling).wait_send())
        return carry

    lax.fori_loop(0, nz * split, drain, 0)


def experts(normed, hidden_state, share, gate_up, down):
    tok, width = normed.shape
    n_dp = lax.axis_size("dp")
    nz, split = n_dp // 2, SPLIT
    rows = tok // split
    units = down.shape[0]
    share = share.reshape(nz, 2, split, rows).transpose(0, 2, 1, 3).reshape(nz, split, 2 * rows, 1)
    vmem = pl.BlockSpec(memory_space=pltpu.VMEM)
    hbm = pl.BlockSpec(memory_space=pl.ANY)
    half = jnp.bfloat16
    dma = pltpu.SemaphoreType.DMA
    out = pl.pallas_call(
        functools.partial(experts_kernel, nz, split),
        out_shape=jax.ShapeDtypeStruct((split, rows, width), half),
        in_specs=[vmem, vmem, vmem, hbm, hbm],
        out_specs=vmem,
        scratch_shapes=[
            pltpu.VMEM(gate_up.shape, half),
            pltpu.VMEM(down.shape, half),
            pltpu.VMEM((nz, split, 2, rows, width), half),
            pltpu.VMEM((nz, split, 2, rows, width), half),
            pltpu.VMEM((nz, split, rows, width), half),
            pltpu.VMEM((2, nz, split, rows, width), half),
            pltpu.VMEM((nz, split, rows, width), half),
            pltpu.VMEM((2 * rows, units), half),
            pltpu.VMEM((rows, width), jnp.float32),
            dma((2,)),
            dma((2, nz, split)),
            dma((nz, split)),
            dma((nz, split)),
            dma((nz, split)),
            dma((nz, split)),
            dma((nz, split)),
            dma((nz, split)),
            dma((2, nz, split)),
        ],
        compiler_params=pltpu.CompilerParams(
            collective_id=1, has_side_effects=True, vmem_limit_bytes=VMEM_BYTES
        ),
        name="experts",
    )(
        normed.reshape(split, rows, width),
        hidden_state.reshape(split, rows, width),
        share, gate_up, down,
    )
    return out.reshape(tok, width)


def attention_kernel(
    nz, plen_ref, q_ref, nk_ref, nv_ref, ck_ref, cv_ref, res_ref, gain_ref, share_ref, w_hbm,
    hidden_ref, normed_ref, shares_ref,
    wb, keys, vals, bias, att, sh,
    load_sem, w_send, w_recv, s_send, s_recv, ssib_send, ssib_recv,
    q_send, q_recv, d_send, d_recv, sw_send, sw_recv,
):
    me, grp = lax.axis_index("dp"), lax.axis_index("grp")
    z, c = me // 2, me % 2
    other = 1 - c
    r = grp % 4
    r1 = r + 1 - 2 * (r % 2)
    r2 = (r + 2) % 4
    r3 = (r1 + 2) % 4
    here, sibling, left, right = (grp, me), (grp, 2 * z + other), (grp, me - 2), (grp, me + 2)
    peers = ((grp - r + r1, me), (grp - r + r2, me))
    has_left, has_right = z > 0, z < nz - 1
    tok, width = q_ref.shape
    cached = ck_ref.shape[0]

    load = pltpu.make_async_copy(w_hbm, wb.at[z, c], load_sem)
    load.start()
    sh[z, c] = share_ref[...]

    barrier = pltpu.get_barrier_semaphore()

    def greet(device):
        pl.semaphore_signal(
            barrier, inc=1, device_id={"grp": device[0], "dp": device[1]},
            device_id_type=pl.DeviceIdType.MESH,
        )

    greet(sibling)
    greet(peers[0])
    greet(peers[1])
    pl.when(has_left)(lambda: greet(left))
    pl.when(has_right)(lambda: greet(right))
    pl.semaphore_wait(barrier, 3 + jnp.where(has_left, 1, 0) + jnp.where(has_right, 1, 0))

    def remote(place, send, recv, device):
        return pltpu.make_async_remote_copy(
            src_ref=place, dst_ref=place, send_sem=send, recv_sem=recv,
            device_id={"grp": device[0], "dp": device[1]}, device_id_type=pl.DeviceIdType.MESH,
        )

    def w_line(b, way, device):
        return remote(wb.at[b, c, r], w_send.at[way, b], w_recv.at[b], device)

    def s_line(b, way, device):
        return remote(sh.at[b, c], s_send.at[way, b], s_recv.at[b], device)

    def s_sib(b, core):
        return remote(sh.at[b, core], ssib_send.at[b], ssib_recv.at[b], sibling)

    def w_sib(b, core, part):
        return remote(wb.at[b, core, part], sw_send.at[b, part], sw_recv.at[b, part], sibling)

    def to_peer(b, peer, part):
        return remote(wb.at[b, c, part], q_send.at[peer, b], q_recv.at[peer, b], peers[peer])

    def corner(b, half, part):
        return remote(
            wb.at[b, c, part, half], d_send.at[half, b], d_recv.at[half, b], peers[1 - half]
        )

    load.wait()
    for way, ok, device in ((0, has_right, right), (1, has_left, left)):

        @pl.when(ok)
        def _(way=way, device=device):
            w_line(z, way, device).start()
            s_line(z, way, device).start()

    s_sib(z, c).start()
    for part in range(4):
        w_sib(z, c, part).start()

    keys[:cached] = ck_ref[...]
    keys[cached:] = nk_ref[...]
    vals[:cached] = cv_ref[...]
    vals[cached:] = nv_ref[...]
    spot = lax.broadcasted_iota(jnp.int32, bias.shape, 1)
    row = lax.broadcasted_iota(jnp.int32, bias.shape, 0)
    seen = (spot < plen_ref[0]) & (spot < cached) | (spot >= cached) & (spot - cached <= row)
    bias[...] = jnp.where(seen, 0.0, NEGATIVE_FILL)
    per_head = HQ // HK // 2

    def attend(t, carry):
        columns = pl.ds(pl.multiple_of(t * 2 * HD, 2 * HD), 2 * HD)
        kv = pl.ds(pl.multiple_of(t // per_head * HD, HD), HD)
        pair = q_ref[:, columns]
        k, v = keys[:, kv], vals[:, kv]
        for h in range(2):
            scores = lax.dot_general(
                pair[:, h * HD : (h + 1) * HD], k, (((1,), (1,)), ((), ())),
                preferred_element_type=jnp.float32,
            ) * HD ** (-0.5) + bias[...]
            probs = jnp.exp(scores - jnp.max(scores, axis=-1, keepdims=True))
            whole = jnp.sum(probs, axis=-1, keepdims=True)
            out = jnp.dot(probs.astype(jnp.bfloat16), v, preferred_element_type=jnp.float32)
            att[:, pl.ds(pl.multiple_of(t * 2 * HD + h * HD, HD), HD)] = (out / whole).astype(
                jnp.bfloat16
            )
        return carry

    def line_step(p):
        b = block_at(p, z, nz)
        w_line(b, 0, sibling).wait_recv()
        s_line(b, 0, sibling).wait_recv()

        @pl.when((b < z) & has_right)
        def _():
            w_line(b, 0, right).start()
            s_line(b, 0, right).start()

        @pl.when((b > z) & has_left)
        def _():
            w_line(b, 1, left).start()
            s_line(b, 1, left).start()

        to_peer(b, 0, r).start()
        to_peer(b, 1, r).start()
        w_sib(b, c, r).start()
        s_sib(b, c).start()

    def peer_step(p):
        b = block_at(p, z, nz)
        to_peer(b, 0, r1).wait_recv()
        corner(b, 0, r1).start()
        w_sib(b, c, r1).start()
        to_peer(b, 1, r2).wait_recv()
        corner(b, 1, r2).start()
        w_sib(b, c, r2).start()

    def corner_step(p):
        b = block_at(p, z, nz)
        corner(b, 0, r3).wait_recv()
        corner(b, 1, r3).wait_recv()
        w_sib(b, c, r3).start()

    steps = HQ // 2
    lax.fori_loop(0, steps // 2, attend, 0)
    line_step(1)
    lax.fori_loop(steps // 2, steps, attend, 0)

    def gather(j, carry):
        pl.when(j < nz)(lambda: line_step(j))
        pl.when(j <= nz)(lambda: peer_step(j - 1))
        pl.when(j > 2)(lambda: corner_step(j - 2))
        return carry

    lax.fori_loop(2, nz + 2, gather, 0)

    hidden_ref[...] = res_ref[...].astype(jnp.float32)
    depth = wb.shape[2] * wb.shape[3] * wb.shape[4]

    def project(p, carry):
        b = block_at(p, z, nz)
        s_sib(b, other).wait_recv()
        for part in range(4):
            w_sib(b, other, part).wait_recv()
        for core in range(2):
            columns = pl.ds(pl.multiple_of((2 * b + core) * depth, 128), depth)
            hidden_ref[...] += jnp.dot(
                att[:, columns], wb[b, core].reshape(depth, wb.shape[5]),
                preferred_element_type=jnp.float32,
            )
        return carry

    lax.fori_loop(0, nz, project, 0)
    hidden_state = hidden_ref[...]
    scale = lax.rsqrt(jnp.mean(hidden_state * hidden_state, axis=-1, keepdims=True) + 1e-06)
    normed_ref[...] = (hidden_state * scale * gain_ref[...]).astype(jnp.bfloat16)
    shares_ref[...] = sh[...]

    def drain(b, carry):
        for way, ok, device in (
            (0, (b <= z) & has_right, right), (1, (b >= z) & has_left, left),
        ):

            @pl.when(ok)
            def _(way=way, device=device):
                w_line(b, way, device).wait_send()
                s_line(b, way, device).wait_send()

        s_sib(b, c).wait_send()
        for part in range(4):
            w_sib(b, c, part).wait_send()

        @pl.when(b != z)
        def _():
            to_peer(b, 0, r).wait_send()
            to_peer(b, 1, r).wait_send()
            corner(b, 0, r1).wait_send()
            corner(b, 1, r2).wait_send()

        return carry

    lax.fori_loop(0, nz, drain, 0)


def attention(
    queries, new_keys, new_values, cache_keys, cache_values, prefix_len, residual, out_weight,
    norm_gain, share,
):
    tok, width = queries.shape
    count = share.shape[0]
    nz = lax.axis_size("dp") // 2
    piece = out_weight.shape[0] // 8
    columns = out_weight.shape[1]
    every = cache_keys.shape[0] + tok
    vmem = pl.BlockSpec(memory_space=pltpu.VMEM)
    half = jnp.bfloat16
    dma = pltpu.SemaphoreType.DMA
    return pl.pallas_call(
        functools.partial(attention_kernel, nz),
        out_shape=(
            jax.ShapeDtypeStruct((tok, columns), jnp.float32),
            jax.ShapeDtypeStruct((tok, columns), half),
            jax.ShapeDtypeStruct((nz, 2, count, tok), jnp.float32),
        ),
        in_specs=[pl.BlockSpec(memory_space=pltpu.SMEM)] + [vmem] * 8
        + [pl.BlockSpec(memory_space=pl.ANY)],
        out_specs=(vmem, vmem, vmem),
        scratch_shapes=[
            pltpu.VMEM((nz, 2, 4, 2, piece, columns), half),
            pltpu.VMEM((every, HK * HD), half),
            pltpu.VMEM((every, HK * HD), half),
            pltpu.VMEM((tok, every), jnp.float32),
            pltpu.VMEM((tok, width), half),
            pltpu.VMEM((nz, 2, count, tok), jnp.float32),
            dma,
            dma((2, nz)), dma((nz,)),
            dma((2, nz)), dma((nz,)),
            dma((nz,)), dma((nz,)),
            dma((2, nz)), dma((2, nz)),
            dma((2, nz)), dma((2, nz)),
            dma((nz, 4)), dma((nz, 4)),
        ],
        compiler_params=pltpu.CompilerParams(
            collective_id=2, has_side_effects=True, vmem_limit_bytes=VMEM_BYTES
        ),
        name="attention",
    )(
        prefix_len, queries, new_keys, new_values, cache_keys, cache_values, residual,
        norm_gain.reshape(1, columns), share, out_weight.reshape(4, 2, piece, columns),
    )


def local(
    queries,
    new_keys,
    new_values,
    cache_keys,
    cache_values,
    prefix_len,
    residual,
    out_weight,
    norm_gain,
    expert_ids,
    gate_scores,
    expert_gate_up,
    expert_down,
):
    count = expert_gate_up.shape[0] * lax.axis_size("dp")
    route_weights = gate_scores / jnp.sum(gate_scores, axis=-1, keepdims=True)
    chosen = expert_ids[:, :, None] == jnp.arange(count, dtype=jnp.int32)
    share = jnp.sum(jnp.where(chosen, route_weights[:, :, None], 0.0), axis=1).T
    hidden_state, normed, shares = attention(
        queries, new_keys, new_values, cache_keys, cache_values, prefix_len, residual, out_weight,
        norm_gain, share,
    )
    share = lax.dynamic_index_in_dim(shares, lax.axis_index("dp"), 2, keepdims=False)
    return experts(normed, hidden_state, share, expert_gate_up[0], expert_down[0])


def solution(mesh):
    in_specs = (
        P(("grp", "dp"), None),
        P(("grp", "dp"), None),
        P(("grp", "dp"), None),
        P(("grp", "dp"), None),
        P(("grp", "dp"), None),
        P(("grp", "dp")),
        P(("grp", "dp"), None),
        P("dp", None),
        P(),
        P(("grp", "dp"), None),
        P(("grp", "dp"), None),
        P("dp", None, None),
        P("dp", None, None),
    )
    out_specs = P(("grp", "dp"), None)
    return jax.shard_map(local, mesh=mesh, in_specs=in_specs, out_specs=out_specs, check_vma=False)
```

```python
import functools

import jax
import jax.numpy as jnp
from jax import lax
from jax.experimental import pallas as pl
from jax.experimental.pallas import tpu as pltpu
from jax.sharding import PartitionSpec as P

D = 2048
HQ = 16
HK = 2
HD = 128
FF = 768
NEGATIVE_FILL = -1e30
SPLIT = 2
VMEM_BYTES = 58 * 1024 * 1024


def block_at(p, z, nz):
    both = jnp.minimum(z, nz - 1 - z)
    half = (p + 1) // 2
    near = jnp.where(p % 2 == 1, z - half, z + half)
    far = jnp.where(z > nz - 1 - z, z - (p - both), z + (p - both))
    return jnp.where(p <= 2 * both, near, far)


def experts_kernel(
    nz, split, x_ref, hidden_ref, share_ref, gu_hbm, down_hbm, out_ref,
    gu, down, xs, ys, sib_sum, line_sum, total, act, acc,
    load_sem, x_send, x_recv, xsib_send, xsib_recv, ysib_send, ysib_recv, line_send, line_recv,
):
    me = lax.axis_index("dp")
    z, c = me // 2, me % 2
    other = 1 - c
    sibling = 2 * z + other
    right, left = me + 2, me - 2
    rows = xs.shape[3]
    width = xs.shape[4]
    hidden_units = down.shape[0]
    has_left, has_right = z > 0, z < nz - 1

    load_gu = pltpu.make_async_copy(gu_hbm, gu, load_sem.at[0])
    load_down = pltpu.make_async_copy(down_hbm, down, load_sem.at[1])
    load_gu.start()
    load_down.start()
    for s in range(split):
        xs[z, s, c] = x_ref[s]

    barrier = pltpu.get_barrier_semaphore()

    def greet(device):
        pl.semaphore_signal(
            barrier, inc=1, device_id={"dp": device}, device_id_type=pl.DeviceIdType.MESH
        )

    greet(sibling)
    pl.when(has_left)(lambda: greet(left))
    pl.when(has_right)(lambda: greet(right))
    pl.semaphore_wait(barrier, 1 + jnp.where(has_left, 1, 0) + jnp.where(has_right, 1, 0))

    def remote(src, dst, send, recv, device):
        return pltpu.make_async_remote_copy(
            src_ref=src, dst_ref=dst, send_sem=send, recv_sem=recv,
            device_id={"dp": device}, device_id_type=pl.DeviceIdType.MESH,
        )

    def x_line(b, s, way, device):
        return remote(xs.at[b, s, c], xs.at[b, s, c], x_send.at[way, b, s], x_recv.at[b, s], device)

    def x_sib(b, s, core):
        return remote(
            xs.at[b, s, core], xs.at[b, s, core], xsib_send.at[b, s], xsib_recv.at[b, s], sibling
        )

    def y_sib(b, s):
        return remote(
            ys.at[b, s, other], sib_sum.at[b, s], ysib_send.at[b, s], ysib_recv.at[b, s], sibling
        )

    def sum_line(b, s, way, device):
        return remote(
            total.at[b, s], line_sum.at[way, b, s], line_send.at[b, s], line_recv.at[way, b, s], device
        )

    def send_sum(b, s):
        pl.when(b > z)(lambda: sum_line(b, s, 0, right).start())
        pl.when(b < z)(lambda: sum_line(b, s, 1, left).start())

    def is_end(b):
        return ((b > z) & (z == 0)) | ((b < z) & (z == nz - 1))

    mirror = nz - 1 - z

    def send_half(s, ok_right, ok_left):
        pl.when(has_right & ok_right)(lambda: x_line(z, s, 0, right).start())
        pl.when(has_left & ok_left)(lambda: x_line(z, s, 1, left).start())

    send_half(0, True, True)
    x_sib(z, 0, c).start()
    x_sib(z, 1, c).start()

    def compute(i, carry):
        slot, side, s = i // 4, i % 2, i // 2 % 2
        pl.when(i % 4 == 0)(lambda: send_half(1, slot == 2 * z + 1, slot == 2 * mirror + 1))
        reach = jnp.where(side == 0, z, mirror)
        near = jnp.where(s == 0, reach - slot, slot - 1 - reach)
        b = jnp.where(slot == 0, z, jnp.where(side == 0, near, nz - 1 - near))
        due = jnp.where(slot == 0, side == 0, (near >= 0) & (near < reach))
        pl.when(due)(lambda: compute_block(slot, b, s))
        return carry

    def compute_block(slot, b, s):
        @pl.when(slot > 0)
        def _():
            x_line(b, s, 0, sibling).wait_recv()
            pl.when((b < z) & has_right)(lambda: x_line(b, s, 0, right).start())
            pl.when((b > z) & has_left)(lambda: x_line(b, s, 1, left).start())
            x_sib(b, s, c).start()

        @pl.when((slot == 0) & (s == 0))
        def _():
            load_gu.wait()
            load_down.wait()

        x_sib(b, s, other).wait_recv()
        x = xs[b, s].reshape(2 * rows, width)
        tile = 256
        for f in range(0, hidden_units, tile):
            gate = jnp.dot(x, gu[:, f : f + tile], preferred_element_type=jnp.float32)
            up = jnp.dot(
                x, gu[:, hidden_units + f : hidden_units + f + tile],
                preferred_element_type=jnp.float32,
            )
            act[:, f : f + tile] = (gate / (1.0 + jnp.exp(-gate)) * up).astype(jnp.bfloat16)
        share = share_ref[b, s]
        for d in range(0, width, 512):
            y = jnp.dot(act[...], down[:, d : d + 512], preferred_element_type=jnp.float32)
            ys[b, s, :, :, d : d + 512] = (
                (y * share).astype(jnp.bfloat16).reshape(2, rows, 512)
            )
        y_sib(b, s).start()

        @pl.when(is_end(b))
        def _():
            y_sib(b, s).wait_recv()
            total[b, s] = (
                ys[b, s, c].astype(jnp.float32) + sib_sum[b, s].astype(jnp.float32)
            ).astype(jnp.bfloat16)
            send_sum(b, s)

    lax.fori_loop(0, 4 * (2 * nz - 1), compute, 0)

    def add_and_pass(b, s, way):
        y_sib(b, s).wait_recv()
        sum_line(b, s, way, sibling).wait_recv()
        total[b, s] = (
            ys[b, s, c].astype(jnp.float32)
            + sib_sum[b, s].astype(jnp.float32)
            + line_sum[way, b, s].astype(jnp.float32)
        ).astype(jnp.bfloat16)
        send_sum(b, s)

    def pass_on(i, carry):
        slot, side, s = i // 4, i % 2, i // 2 % 2
        reach = jnp.where(side == 0, z, mirror)
        far = jnp.where(s == 0, slot - reach, 2 * nz - 1 + reach - slot)
        b = jnp.where(side == 0, far, nz - 1 - far)
        due = (reach > 0) & (far > reach) & (far < nz)
        pl.when(due)(lambda: add_and_pass(b, s, side))
        return carry

    lax.fori_loop(4, 4 * 3 * nz, pass_on, 0)

    def finish(s, carry):
        y_sib(z, s).wait_recv()
        acc[...] = (
            hidden_ref[s] + ys[z, s, c].astype(jnp.float32) + sib_sum[z, s].astype(jnp.float32)
        )

        @pl.when(has_left)
        def _():
            sum_line(z, s, 0, sibling).wait_recv()
            acc[...] += line_sum[0, z, s].astype(jnp.float32)

        @pl.when(has_right)
        def _():
            sum_line(z, s, 1, sibling).wait_recv()
            acc[...] += line_sum[1, z, s].astype(jnp.float32)

        out_ref[s] = acc[...].astype(out_ref.dtype)
        return carry

    lax.fori_loop(0, split, finish, 0)

    def drain(i, carry):
        b, s = i // split, i % split
        pl.when((b <= z) & has_right)(lambda: x_line(b, s, 0, right).wait_send())
        pl.when((b >= z) & has_left)(lambda: x_line(b, s, 1, left).wait_send())
        x_sib(b, s, c).wait_send()
        y_sib(b, s).wait_send()
        pl.when(b != z)(lambda: sum_line(b, s, 0, sibling).wait_send())
        return carry

    lax.fori_loop(0, nz * split, drain, 0)


def experts(normed, hidden_state, share, gate_up, down):
    tok, width = normed.shape
    n_dp = lax.axis_size("dp")
    nz, split = n_dp // 2, SPLIT
    rows = tok // split
    units = down.shape[0]
    share = share.reshape(nz, 2, split, rows).transpose(0, 2, 1, 3).reshape(nz, split, 2 * rows, 1)
    vmem = pl.BlockSpec(memory_space=pltpu.VMEM)
    hbm = pl.BlockSpec(memory_space=pl.ANY)
    half = jnp.bfloat16
    dma = pltpu.SemaphoreType.DMA
    out = pl.pallas_call(
        functools.partial(experts_kernel, nz, split),
        out_shape=jax.ShapeDtypeStruct((split, rows, width), half),
        in_specs=[vmem, vmem, vmem, hbm, hbm],
        out_specs=vmem,
        scratch_shapes=[
            pltpu.VMEM(gate_up.shape, half),
            pltpu.VMEM(down.shape, half),
            pltpu.VMEM((nz, split, 2, rows, width), half),
            pltpu.VMEM((nz, split, 2, rows, width), half),
            pltpu.VMEM((nz, split, rows, width), half),
            pltpu.VMEM((2, nz, split, rows, width), half),
            pltpu.VMEM((nz, split, rows, width), half),
            pltpu.VMEM((2 * rows, units), half),
            pltpu.VMEM((rows, width), jnp.float32),
            dma((2,)),
            dma((2, nz, split)),
            dma((nz, split)),
            dma((nz, split)),
            dma((nz, split)),
            dma((nz, split)),
            dma((nz, split)),
            dma((nz, split)),
            dma((2, nz, split)),
        ],
        compiler_params=pltpu.CompilerParams(
            collective_id=1, has_side_effects=True, vmem_limit_bytes=VMEM_BYTES
        ),
        name="experts",
    )(
        normed.reshape(split, rows, width),
        hidden_state.reshape(split, rows, width),
        share, gate_up, down,
    )
    return out.reshape(tok, width)


def attention_kernel(
    nz, plen_ref, q_ref, nk_ref, nv_ref, ck_ref, cv_ref, res_ref, gain_ref, share_ref, w_hbm,
    hidden_ref, normed_ref, shares_ref,
    wb, keys, vals, bias, att, sh,
    load_sem, w_send, w_recv, s_send, s_recv, ssib_send, ssib_recv,
    q_send, q_recv, d_send, d_recv, sw_send, sw_recv,
):
    me, grp = lax.axis_index("dp"), lax.axis_index("grp")
    z, c = me // 2, me % 2
    other = 1 - c
    r = grp % 4
    r1 = r + 1 - 2 * (r % 2)
    r2 = (r + 2) % 4
    r3 = (r1 + 2) % 4
    here, sibling, left, right = (grp, me), (grp, 2 * z + other), (grp, me - 2), (grp, me + 2)
    peers = ((grp - r + r1, me), (grp - r + r2, me))
    has_left, has_right = z > 0, z < nz - 1
    tok, width = q_ref.shape
    cached = ck_ref.shape[0]

    load = pltpu.make_async_copy(w_hbm, wb.at[z, c], load_sem)
    load.start()
    sh[z, c] = share_ref[...]

    barrier = pltpu.get_barrier_semaphore()

    def greet(device):
        pl.semaphore_signal(
            barrier, inc=1, device_id={"grp": device[0], "dp": device[1]},
            device_id_type=pl.DeviceIdType.MESH,
        )

    greet(sibling)
    greet(peers[0])
    greet(peers[1])
    pl.when(has_left)(lambda: greet(left))
    pl.when(has_right)(lambda: greet(right))
    pl.semaphore_wait(barrier, 3 + jnp.where(has_left, 1, 0) + jnp.where(has_right, 1, 0))

    def remote(place, send, recv, device):
        return pltpu.make_async_remote_copy(
            src_ref=place, dst_ref=place, send_sem=send, recv_sem=recv,
            device_id={"grp": device[0], "dp": device[1]}, device_id_type=pl.DeviceIdType.MESH,
        )

    def w_line(b, way, device):
        return remote(wb.at[b, c, r], w_send.at[way, b], w_recv.at[b], device)

    def s_line(b, way, device):
        return remote(sh.at[b, c], s_send.at[way, b], s_recv.at[b], device)

    def s_sib(b, core):
        return remote(sh.at[b, core], ssib_send.at[b], ssib_recv.at[b], sibling)

    def w_sib(b, core, part):
        return remote(wb.at[b, core, part], sw_send.at[b, part], sw_recv.at[b, part], sibling)

    def to_peer(b, peer, part):
        return remote(wb.at[b, c, part], q_send.at[peer, b], q_recv.at[peer, b], peers[peer])

    def corner(b, half, part):
        return remote(
            wb.at[b, c, part, half], d_send.at[half, b], d_recv.at[half, b], peers[1 - half]
        )

    load.wait()
    for way, ok, device in ((0, has_right, right), (1, has_left, left)):

        @pl.when(ok)
        def _(way=way, device=device):
            w_line(z, way, device).start()
            s_line(z, way, device).start()

    s_sib(z, c).start()
    for part in range(4):
        w_sib(z, c, part).start()

    keys[:cached] = ck_ref[...]
    keys[cached:] = nk_ref[...]
    vals[:cached] = cv_ref[...]
    vals[cached:] = nv_ref[...]
    spot = lax.broadcasted_iota(jnp.int32, bias.shape, 1)
    row = lax.broadcasted_iota(jnp.int32, bias.shape, 0)
    seen = (spot < plen_ref[0]) & (spot < cached) | (spot >= cached) & (spot - cached <= row)
    bias[...] = jnp.where(seen, 0.0, NEGATIVE_FILL)
    per_head = HQ // HK // 2

    def attend(t, carry):
        columns = pl.ds(pl.multiple_of(t * 2 * HD, 2 * HD), 2 * HD)
        kv = pl.ds(pl.multiple_of(t // per_head * HD, HD), HD)
        pair = q_ref[:, columns]
        k, v = keys[:, kv], vals[:, kv]
        for h in range(2):
            scores = lax.dot_general(
                pair[:, h * HD : (h + 1) * HD], k, (((1,), (1,)), ((), ())),
                preferred_element_type=jnp.float32,
            ) * HD ** (-0.5) + bias[...]
            probs = jnp.exp(scores - jnp.max(scores, axis=-1, keepdims=True))
            whole = jnp.sum(probs, axis=-1, keepdims=True)
            out = jnp.dot(probs.astype(jnp.bfloat16), v, preferred_element_type=jnp.float32)
            att[:, pl.ds(pl.multiple_of(t * 2 * HD + h * HD, HD), HD)] = (out / whole).astype(
                jnp.bfloat16
            )
        return carry

    def line_step(p):
        b = block_at(p, z, nz)
        w_line(b, 0, sibling).wait_recv()
        s_line(b, 0, sibling).wait_recv()

        @pl.when((b < z) & has_right)
        def _():
            w_line(b, 0, right).start()
            s_line(b, 0, right).start()

        @pl.when((b > z) & has_left)
        def _():
            w_line(b, 1, left).start()
            s_line(b, 1, left).start()

        to_peer(b, 0, r).start()
        to_peer(b, 1, r).start()
        w_sib(b, c, r).start()
        s_sib(b, c).start()

    def peer_step(p):
        b = block_at(p, z, nz)
        to_peer(b, 0, r1).wait_recv()
        corner(b, 0, r1).start()
        w_sib(b, c, r1).start()
        to_peer(b, 1, r2).wait_recv()
        corner(b, 1, r2).start()
        w_sib(b, c, r2).start()

    def corner_step(p):
        b = block_at(p, z, nz)
        corner(b, 0, r3).wait_recv()
        corner(b, 1, r3).wait_recv()
        w_sib(b, c, r3).start()

    steps = HQ // 2
    lax.fori_loop(0, steps // 2, attend, 0)
    line_step(1)
    lax.fori_loop(steps // 2, steps, attend, 0)

    def gather(j, carry):
        pl.when(j < nz)(lambda: line_step(j))
        pl.when(j <= nz)(lambda: peer_step(j - 1))
        pl.when(j > 2)(lambda: corner_step(j - 2))
        return carry

    lax.fori_loop(2, nz + 2, gather, 0)

    hidden_ref[...] = res_ref[...].astype(jnp.float32)
    depth = wb.shape[2] * wb.shape[3] * wb.shape[4]

    def project(p, carry):
        b = block_at(p, z, nz)
        s_sib(b, other).wait_recv()
        for part in range(4):
            w_sib(b, other, part).wait_recv()
        for core in range(2):
            columns = pl.ds(pl.multiple_of((2 * b + core) * depth, 128), depth)
            hidden_ref[...] += jnp.dot(
                att[:, columns], wb[b, core].reshape(depth, wb.shape[5]),
                preferred_element_type=jnp.float32,
            )
        return carry

    lax.fori_loop(0, nz, project, 0)
    hidden_state = hidden_ref[...]
    scale = lax.rsqrt(jnp.mean(hidden_state * hidden_state, axis=-1, keepdims=True) + 1e-06)
    normed_ref[...] = (hidden_state * scale * gain_ref[...]).astype(jnp.bfloat16)
    shares_ref[...] = sh[...]

    def drain(b, carry):
        for way, ok, device in (
            (0, (b <= z) & has_right, right), (1, (b >= z) & has_left, left),
        ):

            @pl.when(ok)
            def _(way=way, device=device):
                w_line(b, way, device).wait_send()
                s_line(b, way, device).wait_send()

        s_sib(b, c).wait_send()
        for part in range(4):
            w_sib(b, c, part).wait_send()

        @pl.when(b != z)
        def _():
            to_peer(b, 0, r).wait_send()
            to_peer(b, 1, r).wait_send()
            corner(b, 0, r1).wait_send()
            corner(b, 1, r2).wait_send()

        return carry

    lax.fori_loop(0, nz, drain, 0)


def attention(
    queries, new_keys, new_values, cache_keys, cache_values, prefix_len, residual, out_weight,
    norm_gain, share,
):
    tok, width = queries.shape
    count = share.shape[0]
    nz = lax.axis_size("dp") // 2
    piece = out_weight.shape[0] // 8
    columns = out_weight.shape[1]
    every = cache_keys.shape[0] + tok
    vmem = pl.BlockSpec(memory_space=pltpu.VMEM)
    half = jnp.bfloat16
    dma = pltpu.SemaphoreType.DMA
    return pl.pallas_call(
        functools.partial(attention_kernel, nz),
        out_shape=(
            jax.ShapeDtypeStruct((tok, columns), jnp.float32),
            jax.ShapeDtypeStruct((tok, columns), half),
            jax.ShapeDtypeStruct((nz, 2, count, tok), jnp.float32),
        ),
        in_specs=[pl.BlockSpec(memory_space=pltpu.SMEM)] + [vmem] * 8
        + [pl.BlockSpec(memory_space=pl.ANY)],
        out_specs=(vmem, vmem, vmem),
        scratch_shapes=[
            pltpu.VMEM((nz, 2, 4, 2, piece, columns), half),
            pltpu.VMEM((every, HK * HD), half),
            pltpu.VMEM((every, HK * HD), half),
            pltpu.VMEM((tok, every), jnp.float32),
            pltpu.VMEM((tok, width), half),
            pltpu.VMEM((nz, 2, count, tok), jnp.float32),
            dma,
            dma((2, nz)), dma((nz,)),
            dma((2, nz)), dma((nz,)),
            dma((nz,)), dma((nz,)),
            dma((2, nz)), dma((2, nz)),
            dma((2, nz)), dma((2, nz)),
            dma((nz, 4)), dma((nz, 4)),
        ],
        compiler_params=pltpu.CompilerParams(
            collective_id=2, has_side_effects=True, vmem_limit_bytes=VMEM_BYTES
        ),
        name="attention",
    )(
        prefix_len, queries, new_keys, new_values, cache_keys, cache_values, residual,
        norm_gain.reshape(1, columns), share, out_weight.reshape(4, 2, piece, columns),
    )


def local(
    queries,
    new_keys,
    new_values,
    cache_keys,
    cache_values,
    prefix_len,
    residual,
    out_weight,
    norm_gain,
    expert_ids,
    gate_scores,
    expert_gate_up,
    expert_down,
):
    count = expert_gate_up.shape[0] * lax.axis_size("dp")
    route_weights = gate_scores / jnp.sum(gate_scores, axis=-1, keepdims=True)
    chosen = expert_ids[:, :, None] == jnp.arange(count, dtype=jnp.int32)
    share = jnp.sum(jnp.where(chosen, route_weights[:, :, None], 0.0), axis=1).T
    hidden_state, normed, shares = attention(
        queries, new_keys, new_values, cache_keys, cache_values, prefix_len, residual, out_weight,
        norm_gain, share,
    )
    share = lax.dynamic_index_in_dim(shares, lax.axis_index("dp"), 2, keepdims=False)
    return experts(normed, hidden_state, share, expert_gate_up[0], expert_down[0])


def solution(mesh):
    in_specs = (
        P(("grp", "dp"), None),
        P(("grp", "dp"), None),
        P(("grp", "dp"), None),
        P(("grp", "dp"), None),
        P(("grp", "dp"), None),
        P(("grp", "dp")),
        P(("grp", "dp"), None),
        P("dp", None),
        P(),
        P(("grp", "dp"), None),
        P(("grp", "dp"), None),
        P("dp", None, None),
        P("dp", None, None),
    )
    out_specs = P(("grp", "dp"), None)
    return jax.shard_map(local, mesh=mesh, in_specs=in_specs, out_specs=out_specs, check_vma=False)
```

```python
import functools

import jax
import jax.numpy as jnp
from jax import lax
from jax.experimental import pallas as pl
from jax.experimental.pallas import tpu as pltpu
from jax.sharding import PartitionSpec as P

D = 2048
HQ = 16
HK = 2
HD = 128
FF = 768
NEGATIVE_FILL = -1e30
SPLIT = 2
VMEM_BYTES = 58 * 1024 * 1024


def block_at(p, z, nz):
    both = jnp.minimum(z, nz - 1 - z)
    half = (p + 1) // 2
    near = jnp.where(p % 2 == 1, z - half, z + half)
    far = jnp.where(z > nz - 1 - z, z - (p - both), z + (p - both))
    return jnp.where(p <= 2 * both, near, far)


def experts_kernel(
    nz, split, x_ref, hidden_ref, share_ref, gu_hbm, down_hbm, out_ref,
    gu, down, xs, ys, sib_sum, line_sum, total, act, acc,
    load_sem, x_send, x_recv, xsib_send, xsib_recv, ysib_send, ysib_recv, line_send, line_recv,
):
    me = lax.axis_index("dp")
    z, c = me // 2, me % 2
    other = 1 - c
    sibling = 2 * z + other
    right, left = me + 2, me - 2
    rows = xs.shape[3]
    width = xs.shape[4]
    hidden_units = down.shape[0]
    has_left, has_right = z > 0, z < nz - 1

    load_gu = pltpu.make_async_copy(gu_hbm, gu, load_sem.at[0])
    load_down = pltpu.make_async_copy(down_hbm, down, load_sem.at[1])
    load_gu.start()
    load_down.start()
    for s in range(split):
        xs[z, s, c] = x_ref[s]

    barrier = pltpu.get_barrier_semaphore()

    def greet(device):
        pl.semaphore_signal(
            barrier, inc=1, device_id={"dp": device}, device_id_type=pl.DeviceIdType.MESH
        )

    greet(sibling)
    pl.when(has_left)(lambda: greet(left))
    pl.when(has_right)(lambda: greet(right))
    pl.semaphore_wait(barrier, 1 + jnp.where(has_left, 1, 0) + jnp.where(has_right, 1, 0))

    def remote(src, dst, send, recv, device):
        return pltpu.make_async_remote_copy(
            src_ref=src, dst_ref=dst, send_sem=send, recv_sem=recv,
            device_id={"dp": device}, device_id_type=pl.DeviceIdType.MESH,
        )

    def x_line(b, s, way, device):
        return remote(xs.at[b, s, c], xs.at[b, s, c], x_send.at[way, b, s], x_recv.at[b, s], device)

    def x_sib(b, s, core):
        return remote(
            xs.at[b, s, core], xs.at[b, s, core], xsib_send.at[b, s], xsib_recv.at[b, s], sibling
        )

    def y_sib(b, s):
        return remote(
            ys.at[b, s, other], sib_sum.at[b, s], ysib_send.at[b, s], ysib_recv.at[b, s], sibling
        )

    def sum_line(b, s, way, device):
        return remote(
            total.at[b, s], line_sum.at[way, b, s], line_send.at[b, s], line_recv.at[way, b, s], device
        )

    def send_sum(b, s):
        pl.when(b > z)(lambda: sum_line(b, s, 0, right).start())
        pl.when(b < z)(lambda: sum_line(b, s, 1, left).start())

    def is_end(b):
        return ((b > z) & (z == 0)) | ((b < z) & (z == nz - 1))

    mirror = nz - 1 - z

    def send_half(s, ok_right, ok_left):
        pl.when(has_right & ok_right)(lambda: x_line(z, s, 0, right).start())
        pl.when(has_left & ok_left)(lambda: x_line(z, s, 1, left).start())

    send_half(0, True, True)
    x_sib(z, 0, c).start()
    x_sib(z, 1, c).start()

    def compute(i, carry):
        slot, side, s = i // 4, i % 2, i // 2 % 2
        pl.when(i % 4 == 0)(lambda: send_half(1, slot == 2 * z + 1, slot == 2 * mirror + 1))
        reach = jnp.where(side == 0, z, mirror)
        near = jnp.where(s == 0, reach - slot, slot - 1 - reach)
        b = jnp.where(slot == 0, z, jnp.where(side == 0, near, nz - 1 - near))
        due = jnp.where(slot == 0, side == 0, (near >= 0) & (near < reach))
        pl.when(due)(lambda: compute_block(slot, b, s))
        return carry

    def compute_block(slot, b, s):
        @pl.when(slot > 0)
        def _():
            x_line(b, s, 0, sibling).wait_recv()
            pl.when((b < z) & has_right)(lambda: x_line(b, s, 0, right).start())
            pl.when((b > z) & has_left)(lambda: x_line(b, s, 1, left).start())
            x_sib(b, s, c).start()

        @pl.when((slot == 0) & (s == 0))
        def _():
            load_gu.wait()
            load_down.wait()

        x_sib(b, s, other).wait_recv()
        x = xs[b, s].reshape(2 * rows, width)
        tile = 256
        for f in range(0, hidden_units, tile):
            gate = jnp.dot(x, gu[:, f : f + tile], preferred_element_type=jnp.float32)
            up = jnp.dot(
                x, gu[:, hidden_units + f : hidden_units + f + tile],
                preferred_element_type=jnp.float32,
            )
            act[:, f : f + tile] = (gate / (1.0 + jnp.exp(-gate)) * up).astype(jnp.bfloat16)
        share = share_ref[b, s]
        for d in range(0, width, 512):
            y = jnp.dot(act[...], down[:, d : d + 512], preferred_element_type=jnp.float32)
            ys[b, s, :, :, d : d + 512] = (
                (y * share).astype(jnp.bfloat16).reshape(2, rows, 512)
            )
        y_sib(b, s).start()

        @pl.when(is_end(b))
        def _():
            y_sib(b, s).wait_recv()
            total[b, s] = (
                ys[b, s, c].astype(jnp.float32) + sib_sum[b, s].astype(jnp.float32)
            ).astype(jnp.bfloat16)
            send_sum(b, s)

    lax.fori_loop(0, 4 * (2 * nz - 1), compute, 0)

    def add_and_pass(b, s, way):
        y_sib(b, s).wait_recv()
        sum_line(b, s, way, sibling).wait_recv()
        total[b, s] = (
            ys[b, s, c].astype(jnp.float32)
            + sib_sum[b, s].astype(jnp.float32)
            + line_sum[way, b, s].astype(jnp.float32)
        ).astype(jnp.bfloat16)
        send_sum(b, s)

    def pass_on(i, carry):
        slot, side, s = i // 4, i % 2, i // 2 % 2
        reach = jnp.where(side == 0, z, mirror)
        far = jnp.where(s == 0, slot - reach, 2 * nz - 1 + reach - slot)
        b = jnp.where(side == 0, far, nz - 1 - far)
        due = (reach > 0) & (far > reach) & (far < nz)
        pl.when(due)(lambda: add_and_pass(b, s, side))
        return carry

    lax.fori_loop(4, 4 * 3 * nz, pass_on, 0)

    def finish(s, carry):
        y_sib(z, s).wait_recv()
        acc[...] = (
            hidden_ref[s] + ys[z, s, c].astype(jnp.float32) + sib_sum[z, s].astype(jnp.float32)
        )

        @pl.when(has_left)
        def _():
            sum_line(z, s, 0, sibling).wait_recv()
            acc[...] += line_sum[0, z, s].astype(jnp.float32)

        @pl.when(has_right)
        def _():
            sum_line(z, s, 1, sibling).wait_recv()
            acc[...] += line_sum[1, z, s].astype(jnp.float32)

        out_ref[s] = acc[...].astype(out_ref.dtype)
        return carry

    lax.fori_loop(0, split, finish, 0)

    def drain(i, carry):
        b, s = i // split, i % split
        pl.when((b <= z) & has_right)(lambda: x_line(b, s, 0, right).wait_send())
        pl.when((b >= z) & has_left)(lambda: x_line(b, s, 1, left).wait_send())
        x_sib(b, s, c).wait_send()
        y_sib(b, s).wait_send()
        pl.when(b != z)(lambda: sum_line(b, s, 0, sibling).wait_send())
        return carry

    lax.fori_loop(0, nz * split, drain, 0)


def experts(normed, hidden_state, share, gate_up, down):
    tok, width = normed.shape
    n_dp = lax.axis_size("dp")
    nz, split = n_dp // 2, SPLIT
    rows = tok // split
    units = down.shape[0]
    share = share.reshape(nz, 2, split, rows).transpose(0, 2, 1, 3).reshape(nz, split, 2 * rows, 1)
    vmem = pl.BlockSpec(memory_space=pltpu.VMEM)
    hbm = pl.BlockSpec(memory_space=pl.ANY)
    half = jnp.bfloat16
    dma = pltpu.SemaphoreType.DMA
    out = pl.pallas_call(
        functools.partial(experts_kernel, nz, split),
        out_shape=jax.ShapeDtypeStruct((split, rows, width), half),
        in_specs=[vmem, vmem, vmem, hbm, hbm],
        out_specs=vmem,
        scratch_shapes=[
            pltpu.VMEM(gate_up.shape, half),
            pltpu.VMEM(down.shape, half),
            pltpu.VMEM((nz, split, 2, rows, width), half),
            pltpu.VMEM((nz, split, 2, rows, width), half),
            pltpu.VMEM((nz, split, rows, width), half),
            pltpu.VMEM((2, nz, split, rows, width), half),
            pltpu.VMEM((nz, split, rows, width), half),
            pltpu.VMEM((2 * rows, units), half),
            pltpu.VMEM((rows, width), jnp.float32),
            dma((2,)),
            dma((2, nz, split)),
            dma((nz, split)),
            dma((nz, split)),
            dma((nz, split)),
            dma((nz, split)),
            dma((nz, split)),
            dma((nz, split)),
            dma((2, nz, split)),
        ],
        compiler_params=pltpu.CompilerParams(
            collective_id=1, has_side_effects=True, vmem_limit_bytes=VMEM_BYTES
        ),
        name="experts",
    )(
        normed.reshape(split, rows, width),
        hidden_state.reshape(split, rows, width),
        share, gate_up, down,
    )
    return out.reshape(tok, width)


def attention_kernel(
    nz, plen_ref, q_ref, nk_ref, nv_ref, ck_ref, cv_ref, res_ref, gain_ref, share_ref, w_hbm,
    hidden_ref, normed_ref, shares_ref,
    wb, keys, vals, bias, att, sh,
    load_sem, w_send, w_recv, s_send, s_recv, ssib_send, ssib_recv,
    q_send, q_recv, d_send, d_recv, sw_send, sw_recv,
):
    me, grp = lax.axis_index("dp"), lax.axis_index("grp")
    z, c = me // 2, me % 2
    other = 1 - c
    r = grp % 4
    r1 = r + 1 - 2 * (r % 2)
    r2 = (r + 2) % 4
    r3 = (r1 + 2) % 4
    here, sibling, left, right = (grp, me), (grp, 2 * z + other), (grp, me - 2), (grp, me + 2)
    peers = ((grp - r + r1, me), (grp - r + r2, me))
    has_left, has_right = z > 0, z < nz - 1
    tok, width = q_ref.shape
    cached = ck_ref.shape[0]

    load = pltpu.make_async_copy(w_hbm, wb.at[z, c], load_sem)
    load.start()
    sh[z, c] = share_ref[...]

    barrier = pltpu.get_barrier_semaphore()

    def greet(device):
        pl.semaphore_signal(
            barrier, inc=1, device_id={"grp": device[0], "dp": device[1]},
            device_id_type=pl.DeviceIdType.MESH,
        )

    greet(sibling)
    greet(peers[0])
    greet(peers[1])
    pl.when(has_left)(lambda: greet(left))
    pl.when(has_right)(lambda: greet(right))
    pl.semaphore_wait(barrier, 3 + jnp.where(has_left, 1, 0) + jnp.where(has_right, 1, 0))

    def remote(place, send, recv, device):
        return pltpu.make_async_remote_copy(
            src_ref=place, dst_ref=place, send_sem=send, recv_sem=recv,
            device_id={"grp": device[0], "dp": device[1]}, device_id_type=pl.DeviceIdType.MESH,
        )

    def w_line(b, way, device):
        return remote(wb.at[b, c, r], w_send.at[way, b], w_recv.at[b], device)

    def s_line(b, way, device):
        return remote(sh.at[b, c], s_send.at[way, b], s_recv.at[b], device)

    def s_sib(b, core):
        return remote(sh.at[b, core], ssib_send.at[b], ssib_recv.at[b], sibling)

    def w_sib(b, core, part):
        return remote(wb.at[b, core, part], sw_send.at[b, part], sw_recv.at[b, part], sibling)

    def to_peer(b, peer, part):
        return remote(wb.at[b, c, part], q_send.at[peer, b], q_recv.at[peer, b], peers[peer])

    def corner(b, half, part):
        return remote(
            wb.at[b, c, part, half], d_send.at[half, b], d_recv.at[half, b], peers[1 - half]
        )

    load.wait()
    for way, ok, device in ((0, has_right, right), (1, has_left, left)):

        @pl.when(ok)
        def _(way=way, device=device):
            w_line(z, way, device).start()
            s_line(z, way, device).start()

    s_sib(z, c).start()
    for part in range(4):
        w_sib(z, c, part).start()

    keys[:cached] = ck_ref[...]
    keys[cached:] = nk_ref[...]
    vals[:cached] = cv_ref[...]
    vals[cached:] = nv_ref[...]
    spot = lax.broadcasted_iota(jnp.int32, bias.shape, 1)
    row = lax.broadcasted_iota(jnp.int32, bias.shape, 0)
    seen = (spot < plen_ref[0]) & (spot < cached) | (spot >= cached) & (spot - cached <= row)
    bias[...] = jnp.where(seen, 0.0, NEGATIVE_FILL)
    per_head = HQ // HK // 2

    def attend(t, carry):
        columns = pl.ds(pl.multiple_of(t * 2 * HD, 2 * HD), 2 * HD)
        kv = pl.ds(pl.multiple_of(t // per_head * HD, HD), HD)
        pair = q_ref[:, columns]
        k, v = keys[:, kv], vals[:, kv]
        for h in range(2):
            scores = lax.dot_general(
                pair[:, h * HD : (h + 1) * HD], k, (((1,), (1,)), ((), ())),
                preferred_element_type=jnp.float32,
            ) * HD ** (-0.5) + bias[...]
            probs = jnp.exp(scores - jnp.max(scores, axis=-1, keepdims=True))
            whole = jnp.sum(probs, axis=-1, keepdims=True)
            out = jnp.dot(probs.astype(jnp.bfloat16), v, preferred_element_type=jnp.float32)
            att[:, pl.ds(pl.multiple_of(t * 2 * HD + h * HD, HD), HD)] = (out / whole).astype(
                jnp.bfloat16
            )
        return carry

    def line_step(p):
        b = block_at(p, z, nz)
        w_line(b, 0, sibling).wait_recv()
        s_line(b, 0, sibling).wait_recv()

        @pl.when((b < z) & has_right)
        def _():
            w_line(b, 0, right).start()
            s_line(b, 0, right).start()

        @pl.when((b > z) & has_left)
        def _():
            w_line(b, 1, left).start()
            s_line(b, 1, left).start()

        to_peer(b, 0, r).start()
        to_peer(b, 1, r).start()
        w_sib(b, c, r).start()
        s_sib(b, c).start()

    def peer_step(p):
        b = block_at(p, z, nz)
        to_peer(b, 0, r1).wait_recv()
        corner(b, 0, r1).start()
        w_sib(b, c, r1).start()
        to_peer(b, 1, r2).wait_recv()
        corner(b, 1, r2).start()
        w_sib(b, c, r2).start()

    def corner_step(p):
        b = block_at(p, z, nz)
        corner(b, 0, r3).wait_recv()
        corner(b, 1, r3).wait_recv()
        w_sib(b, c, r3).start()

    steps = HQ // 2
    lax.fori_loop(0, steps // 2, attend, 0)
    line_step(1)
    lax.fori_loop(steps // 2, steps, attend, 0)

    hidden_ref[...] = res_ref[...].astype(jnp.float32)
    depth = wb.shape[2] * wb.shape[3] * wb.shape[4]

    def project(p):
        b = block_at(p, z, nz)
        s_sib(b, other).wait_recv()
        for part in range(4):
            w_sib(b, other, part).wait_recv()
        for core in range(2):
            columns = pl.ds(pl.multiple_of((2 * b + core) * depth, 128), depth)
            hidden_ref[...] += jnp.dot(
                att[:, columns], wb[b, core].reshape(depth, wb.shape[5]),
                preferred_element_type=jnp.float32,
            )

    def gather(j, carry):
        pl.when(j < nz)(lambda: line_step(j))
        pl.when(j <= nz)(lambda: peer_step(j - 1))
        pl.when(j > 2)(lambda: corner_step(j - 2))
        pl.when(j > 2)(lambda: project(j - 3))
        return carry

    lax.fori_loop(2, nz + 2, gather, 0)
    project(nz - 1)
    hidden_state = hidden_ref[...]
    scale = lax.rsqrt(jnp.mean(hidden_state * hidden_state, axis=-1, keepdims=True) + 1e-06)
    normed_ref[...] = (hidden_state * scale * gain_ref[...]).astype(jnp.bfloat16)
    shares_ref[...] = sh[...]

    def drain(b, carry):
        for way, ok, device in (
            (0, (b <= z) & has_right, right), (1, (b >= z) & has_left, left),
        ):

            @pl.when(ok)
            def _(way=way, device=device):
                w_line(b, way, device).wait_send()
                s_line(b, way, device).wait_send()

        s_sib(b, c).wait_send()
        for part in range(4):
            w_sib(b, c, part).wait_send()

        @pl.when(b != z)
        def _():
            to_peer(b, 0, r).wait_send()
            to_peer(b, 1, r).wait_send()
            corner(b, 0, r1).wait_send()
            corner(b, 1, r2).wait_send()

        return carry

    lax.fori_loop(0, nz, drain, 0)


def attention(
    queries, new_keys, new_values, cache_keys, cache_values, prefix_len, residual, out_weight,
    norm_gain, share,
):
    tok, width = queries.shape
    count = share.shape[0]
    nz = lax.axis_size("dp") // 2
    piece = out_weight.shape[0] // 8
    columns = out_weight.shape[1]
    every = cache_keys.shape[0] + tok
    vmem = pl.BlockSpec(memory_space=pltpu.VMEM)
    half = jnp.bfloat16
    dma = pltpu.SemaphoreType.DMA
    return pl.pallas_call(
        functools.partial(attention_kernel, nz),
        out_shape=(
            jax.ShapeDtypeStruct((tok, columns), jnp.float32),
            jax.ShapeDtypeStruct((tok, columns), half),
            jax.ShapeDtypeStruct((nz, 2, count, tok), jnp.float32),
        ),
        in_specs=[pl.BlockSpec(memory_space=pltpu.SMEM)] + [vmem] * 8
        + [pl.BlockSpec(memory_space=pl.ANY)],
        out_specs=(vmem, vmem, vmem),
        scratch_shapes=[
            pltpu.VMEM((nz, 2, 4, 2, piece, columns), half),
            pltpu.VMEM((every, HK * HD), half),
            pltpu.VMEM((every, HK * HD), half),
            pltpu.VMEM((tok, every), jnp.float32),
            pltpu.VMEM((tok, width), half),
            pltpu.VMEM((nz, 2, count, tok), jnp.float32),
            dma,
            dma((2, nz)), dma((nz,)),
            dma((2, nz)), dma((nz,)),
            dma((nz,)), dma((nz,)),
            dma((2, nz)), dma((2, nz)),
            dma((2, nz)), dma((2, nz)),
            dma((nz, 4)), dma((nz, 4)),
        ],
        compiler_params=pltpu.CompilerParams(
            collective_id=2, has_side_effects=True, vmem_limit_bytes=VMEM_BYTES
        ),
        name="attention",
    )(
        prefix_len, queries, new_keys, new_values, cache_keys, cache_values, residual,
        norm_gain.reshape(1, columns), share, out_weight.reshape(4, 2, piece, columns),
    )


def local(
    queries,
    new_keys,
    new_values,
    cache_keys,
    cache_values,
    prefix_len,
    residual,
    out_weight,
    norm_gain,
    expert_ids,
    gate_scores,
    expert_gate_up,
    expert_down,
):
    count = expert_gate_up.shape[0] * lax.axis_size("dp")
    route_weights = gate_scores / jnp.sum(gate_scores, axis=-1, keepdims=True)
    chosen = expert_ids[:, :, None] == jnp.arange(count, dtype=jnp.int32)
    share = jnp.sum(jnp.where(chosen, route_weights[:, :, None], 0.0), axis=1).T
    hidden_state, normed, shares = attention(
        queries, new_keys, new_values, cache_keys, cache_values, prefix_len, residual, out_weight,
        norm_gain, share,
    )
    share = lax.dynamic_index_in_dim(shares, lax.axis_index("dp"), 2, keepdims=False)
    return experts(normed, hidden_state, share, expert_gate_up[0], expert_down[0])


def solution(mesh):
    in_specs = (
        P(("grp", "dp"), None),
        P(("grp", "dp"), None),
        P(("grp", "dp"), None),
        P(("grp", "dp"), None),
        P(("grp", "dp"), None),
        P(("grp", "dp")),
        P(("grp", "dp"), None),
        P("dp", None),
        P(),
        P(("grp", "dp"), None),
        P(("grp", "dp"), None),
        P("dp", None, None),
        P("dp", None, None),
    )
    out_specs = P(("grp", "dp"), None)
    return jax.shard_map(local, mesh=mesh, in_specs=in_specs, out_specs=out_specs, check_vma=False)
```
